32 devices in a mesh: ctx: 8 (over z, x), head: 4 (over y, core).
Axes of the slice: x: 2, y: 2, z: 4, core: 2. Of those that a mesh axis runs over, the one named last changes fastest.
Arguments:
- latent: bfloat16 [2048, 576], P('ctx'), may hold values from -8 to 8
- query: bfloat16 [2048, 12288], P('ctx', 'head'), may hold values from -300 to 300
- d_out: bfloat16 [2048, 8192], P('ctx', 'head'), may hold values from -6 to 6
- w_uk: bfloat16 [64, 128, 512], P('head'), may hold values from -0.5 to 0.5
- w_uv: bfloat16 [64, 128, 512], P('head'), may hold values from -0.25 to 0.25
- block_mask: int32 [8, 8], replicated, may hold values 0 or 1
- segments: int32 [2048], replicated, may hold values from 0 to 3, never falling along the last dimension, each value on 1 to 1536 neighbouring positions
Outputs:
- attended: bfloat16 [2048, 8192], P('ctx', 'head')
- d_query: bfloat16 [2048, 12288], P('ctx', 'head')
- d_latent: float32 [2048, 576], P('ctx')
- d_w_uk: float32 [64, 128, 512], P('head')
- d_w_uv: float32 [64, 128, 512], P('head')
The draws below stay inside these ranges and needn't reach their ends.
Inputs may be any that keep to these rules, and one draw needn't show every extreme that they name: block_mask[a, b] = 1 lets every token of block a read every earlier token of block b whatever their dialogues. `segments`: dialogue ids never fall along the sequence; each dialogue holds 1 to 1536 tokens and one holds exactly 1536.
All inputs are finite; a program needn't handle non-finite values.
Results may differ from the reference program's by a relative error of at most 0.012.
The reference program's roundings to bfloat16 on the way (of `q_nope`, `absorbed`, `q_full`, `probs_low`, `latent_out`, `d_latent_out`, `d_scores` and `d_absorbed`) count: a program that leaves them out, or rounds other values in their place, can miss the bound.
Values may be sent and summed in bfloat16 or wider, within the bound.
A program may use at most 256 MiB of HBM per device.

```python
import math
import jax
import jax.numpy as jnp
import numpy as np
from jax import lax

TOK_DEV = 256
HEADS = 64
NOPE = 128
ROPE = 64
RANK = 512
VDIM = 128
SPAN = 2
LAT = 576
QW = 192
TOKENS = 2048
NSEG = 4
N_CTX = 8


def shared_rope(key):
    return jnp.clip(jax.random.normal(key, (TOKENS, ROPE), jnp.float32), -4.0, 4.0)


def draw_latent(key, part):
    key_rope = shared_rope(key)
    key = jax.random.fold_in(key, 3)
    key_values = jax.random.fold_in(key, 0)
    values = jnp.clip(jax.random.normal(key_values, (TOKENS, RANK), jnp.float32), -4.0, 4.0)
    return jnp.concatenate([values, key_rope], axis=1).astype(jnp.bfloat16)


def draw_query(key, part):
    key = jax.random.fold_in(key, 5)
    key_values = jax.random.fold_in(key, 0)
    whole_query = jnp.clip(jax.random.normal(key_values, (TOKENS, HEADS, QW), jnp.float32), -4.0, 4.0)
    return whole_query.reshape(TOKENS, HEADS * QW).astype(jnp.bfloat16)


def with_ends(array, stream_key, smallest, top_value):
    index_at = [jax.random.randint(jax.random.fold_in(stream_key, axis), (), 0, length) for axis, length in enumerate(array.shape)]
    main_axis = array.shape.index(max(array.shape))
    next_to = index_at[:main_axis] + [(index_at[main_axis] + 1) % array.shape[main_axis]] + index_at[main_axis + 1:]
    return array.at[tuple(index_at)].set(smallest).at[tuple(next_to)].set(top_value)


def steps_of(own_key, dims, cuts, least, high):
    gain, own = 1.0, jax.random.fold_in(own_key, 6)
    for dim, shards_of in cuts:
        draws = jnp.exp(jax.random.uniform(jax.random.fold_in(own, dim), (shards_of,), jnp.float32, least / len(cuts), high / len(cuts)))
        gain = gain * jnp.repeat(draws, dims[dim] // shards_of).reshape([-1 if axis == dim else 1 for axis in range(len(dims))])
    return gain


def split_up(count, total, most, lean):
    loads = [(1 << 20) // math.isqrt(standing ** lean) + 1 for standing in range(2, count + 1)]
    surplus, counts = total - most - (count - 1), [1] * (count - 1)
    while surplus > 0:
        movable = [i for i in range(count - 1) if counts[i] < most]
        pool, remaining = sum([loads[i] for i in movable]), surplus
        for i in movable:
            extra = min(most - counts[i], max(1, remaining * loads[i] // pool), surplus)
            counts[i] = counts[i] + extra
            surplus = surplus - extra
    return np.array([most] + counts)


def uneven(key, number_of, total, limit, lean):
    if number_of == 2:
        one = jax.random.randint(key, (), max(1, total - limit), min(limit, total - 1) + 1)
        return jnp.stack([one, total - one])
    sizes = jnp.asarray(split_up(number_of, total, limit, lean), jnp.int32)
    couples = (number_of - 1) // 2
    source_of, sink = sizes[1:1 + 2 * couples:2], sizes[2:2 + 2 * couples:2]
    room = jnp.minimum(source_of - 1, limit - sink)
    passed = jax.random.randint(jax.random.fold_in(key, 1), (couples,), 0, 1 << 20) % (room + 1)
    sizes = sizes.at[1:1 + 2 * couples:2].set(source_of - passed).at[2:2 + 2 * couples:2].set(sink + passed)
    return sizes[jax.random.permutation(jax.random.fold_in(key, 2), number_of)]


def noise(own_key, dims, scale, limit, shards=(), held_as=jnp.bfloat16):
    drawn = jax.random.normal(own_key, dims, jnp.float32) * scale
    if len(shards) > 0:
        drawn = steps_of(own_key, dims, shards, -0.22, 0.18) * drawn
    return jnp.clip(drawn, min=-limit, max=limit).astype(held_as)


def setup_inputs(seed: int = 0) -> dict:
    seeds = jax.random.split(jax.random.key(seed), 8)
    return {
        "latent": draw_latent(jax.random.fold_in(seeds[7], 71), 0),
        "query": draw_query(jax.random.fold_in(seeds[7], 71), 0),
        "d_out": noise(seeds[2], (TOKENS, HEADS * VDIM), 1.0, 6.0, ((0, 8), (1, 4))),
        "w_uk": noise(seeds[3], (HEADS, NOPE, RANK), NOPE ** -0.5, 0.5, ((0, 4),)),
        "w_uv": noise(seeds[4], (HEADS, VDIM, RANK), RANK ** -0.5, 0.25, ((0, 4),)),
        "block_mask": with_ends((jax.random.randint(seeds[5], (N_CTX, N_CTX), 0, 2) < 1).astype(jnp.int32), jax.random.fold_in(seeds[5], 1), 0, 1),
        "segments": jnp.searchsorted(jnp.cumsum(uneven(seeds[6], NSEG, TOKENS, 6 * TOK_DEV, 0)), jnp.arange(TOKENS), side="right").astype(jnp.int32),
    }


def rounded(values):
    return lax.optimization_barrier(values.astype(jnp.bfloat16))

def widen(values):
    return values.astype(jnp.float32)

def reference(latent, query, d_out, w_uk, w_uv, block_mask, segments):
    inv_root = 1.0 / math.sqrt(QW)
    queries = query.reshape(TOKENS, HEADS, QW)
    grads_all = d_out.reshape(TOKENS, HEADS, VDIM)
    padded = jnp.concatenate([jnp.zeros((SPAN * TOK_DEV, LAT), latent.dtype), latent], axis=0)
    seg_padded = jnp.concatenate([jnp.zeros((SPAN * TOK_DEV,), jnp.int32), segments.astype(jnp.int32)], axis=0)
    w_uk_wide = widen(w_uk)
    w_uv_wide = widen(w_uv)
    width = (SPAN + 1) * TOK_DEV
    offsets_q = jnp.arange(TOK_DEV, dtype=jnp.int32)
    offsets_k = jnp.arange(width, dtype=jnp.int32)

    def query_block(carried, block_id):
        d_keys_all, grad_uk, grad_uv = carried
        start = (block_id * TOK_DEV).astype(jnp.int32)
        q_here = lax.dynamic_slice_in_dim(queries, start, TOK_DEV, 0)
        q_nope = q_here[:, :, :NOPE]
        q_rope = q_here[:, :, NOPE:]
        absorbed = rounded(jnp.einsum('thn,hnr->thr', widen(q_nope), w_uk_wide))
        q_full = jnp.concatenate([absorbed, q_rope], axis=2)
        keys = lax.dynamic_slice_in_dim(padded, start, width, 0)
        content = keys[:, :RANK]
        seg_keys = lax.dynamic_slice_in_dim(seg_padded, start, width, 0)
        seg_query = lax.dynamic_slice_in_dim(segments.astype(jnp.int32), start, TOK_DEV, 0)
        key_block = block_id - SPAN + offsets_k // TOK_DEV
        granted = block_mask[block_id, jnp.maximum(key_block, 0)]
        q_pos = start + offsets_q
        k_pos = start - SPAN * TOK_DEV + offsets_k
        allowed = (key_block >= 0)[None, :] & (k_pos[None, :] <= q_pos[:, None]) & ((seg_query[:, None] == seg_keys[None, :]) | (granted == 1)[None, :])
        scores = jnp.einsum('thl,kl->htk', widen(q_full), widen(keys)) * inv_root
        scores = jnp.where(allowed[None], scores, -jnp.inf)
        row_max = lax.optimization_barrier(jnp.max(scores, axis=2, keepdims=True))
        weights = jnp.exp(scores - row_max)
        probs = weights / lax.optimization_barrier(jnp.sum(weights, axis=2, keepdims=True))
        probs_low = rounded(probs)
        latent_out = rounded(jnp.einsum('htk,kr->thr', widen(probs_low), widen(content)))
        attended = jnp.einsum('thr,hvr->thv', widen(latent_out), w_uv_wide).astype(jnp.bfloat16)
        grads = lax.dynamic_slice_in_dim(grads_all, start, TOK_DEV, 0)
        d_latent_out = rounded(jnp.einsum('thv,hvr->thr', widen(grads), w_uv_wide))
        grad_uv = grad_uv + jnp.einsum('thv,thr->hvr', widen(grads), widen(latent_out))
        d_probs = jnp.einsum('thr,kr->htk', widen(d_latent_out), widen(content))
        delta = lax.optimization_barrier(jnp.sum(probs * d_probs, axis=2, keepdims=True))
        d_scores = rounded(probs * (d_probs - delta) * inv_root)
        d_full = jnp.einsum('htk,kl->thl', widen(d_scores), widen(keys))
        d_absorbed = rounded(d_full[:, :, :RANK])
        d_nope = jnp.einsum('thr,hnr->thn', widen(d_absorbed), w_uk_wide)
        d_query = jnp.concatenate([d_nope, d_full[:, :, RANK:]], axis=2).astype(jnp.bfloat16)
        grad_uk = grad_uk + jnp.einsum('thn,thr->hnr', widen(q_nope), widen(d_absorbed))
        d_keys = jnp.einsum('htk,thl->kl', widen(d_scores), widen(q_full)) + jnp.pad(jnp.einsum('htk,thr->kr', widen(probs_low), widen(d_latent_out)), ((0, 0), (0, ROPE)))
        previous = lax.dynamic_slice_in_dim(d_keys_all, start, width, 0)
        d_keys_all = lax.dynamic_update_slice_in_dim(d_keys_all, previous + d_keys, start, 0)
        return ((d_keys_all, grad_uk, grad_uv), (attended.reshape(TOK_DEV, HEADS * VDIM), d_query.reshape(TOK_DEV, HEADS * QW)))
    initial = (jnp.zeros(((N_CTX + SPAN) * TOK_DEV, LAT), jnp.float32), jnp.zeros((HEADS, NOPE, RANK), jnp.float32), jnp.zeros((HEADS, VDIM, RANK), jnp.float32))
    finals, stacked = lax.scan(query_block, initial, jnp.arange(N_CTX, dtype=jnp.int32))
    d_keys_all, grad_uk, grad_uv = finals
    attended, d_query = stacked
    return (attended.reshape(TOKENS, HEADS * VDIM), d_query.reshape(TOKENS, HEADS * QW), d_keys_all[SPAN * TOK_DEV:], grad_uk, grad_uv)
```

```python
import functools
import math

import jax
import jax.numpy as jnp
from jax import lax
from jax.experimental import pallas as pl
from jax.experimental.pallas import tpu as pltpu
from jax.sharding import PartitionSpec as P

SPAN = 2
PAIR = 2
CHUNKS = 4


def dot(a, b):
    return lax.dot_general(a, b, (((1,), (0,)), ((), ())), preferred_element_type=jnp.float32)


def dot_t(a, b):
    return lax.dot_general(a, b, (((1,), (1,)), ((), ())), preferred_element_type=jnp.float32)


def attention_kernel(
    nope, rope, rank, value,
    keys_ref, keys_t_ref, bias_ref, query_ref, grads_ref, uk_ref, uv_ref, *rest,
):
    att_ref, dq_ref, dkeys_ref, duk_ref, duv_ref = rest[-5:]
    bf16 = jnp.bfloat16
    width = nope + rope
    inv_root = 1.0 / math.sqrt(width)
    to_log2 = inv_root * math.log2(math.e)

    @pl.when(pl.program_id(0) == 0)
    def _():
        dkeys_ref[...] = jnp.zeros_like(dkeys_ref)

    queries = query_ref[...]
    for head in range(PAIR):
        q_nope = queries[:, head * width : head * width + nope]
        q_rope = queries[:, head * width + nope : (head + 1) * width]
        grads = grads_ref[:, head * value : (head + 1) * value]
        w_uk = uk_ref[head]
        w_uv = uv_ref[head]
        absorbed = dot(q_nope, w_uk).astype(bf16)
        d_out_latent = dot(grads, w_uv).astype(bf16)
        content = keys_ref[:, :rank]
        scores = dot_t(content, absorbed) + dot_t(keys_ref[:, rank:], q_rope)
        scores = scores * to_log2 + bias_ref[...]
        weights = jnp.exp2(scores - jnp.max(scores, axis=0, keepdims=True))
        probs = weights * (1.0 / jnp.sum(weights, axis=0, keepdims=True))
        low = probs.astype(bf16)
        out_t = dot(keys_t_ref[:rank, :], low).astype(bf16)
        att_t = dot(w_uv, out_t)
        att_ref[:, head * value : (head + 1) * value] = att_t.T.astype(bf16)
        duv_ref[head] = dot_t(grads.T, out_t).astype(duv_ref.dtype)
        d_probs = dot_t(content, d_out_latent)
        delta = jnp.sum(probs * d_probs, axis=0, keepdims=True)
        d_scores = (probs * (d_probs - delta) * inv_root).astype(bf16)
        d_full_t = dot(keys_t_ref[...], d_scores)
        d_absorbed_t = d_full_t[:rank].astype(bf16)
        d_nope_t = dot(w_uk, d_absorbed_t)
        dq_ref[:, head * width : (head + 1) * width] = jnp.concatenate(
            [d_nope_t, d_full_t[rank:]], axis=0
        ).T.astype(bf16)
        duk_ref[head] = dot_t(q_nope.T, d_absorbed_t).astype(duk_ref.dtype)
        dkeys_ref[:, :rank] += dot(d_scores, absorbed) + dot(low, d_out_latent)
        dkeys_ref[:, rank:] += dot(d_scores, q_rope)


def attend(chunk, chunks, keys, keys_t, bias, query, d_out, w_uk, w_uv, *filled):
    tok = query.shape[0]
    heads, nope, rank = w_uk.shape
    value = w_uv.shape[1]
    width = query.shape[1] // heads
    lat = keys.shape[1]
    span = keys.shape[0]
    steps = heads // chunks // PAIR
    first = chunk * steps
    fixed = lambda i: (0, 0)
    columns = lambda i: (0, first + i)
    weight = lambda i: (first + i, 0, 0)
    own = lambda i: (i, 0, 0)
    here = steps * PAIR
    flops = 2 * tok * here * (span * (3 * lat + 3 * rank) + 6 * nope * rank)
    return pl.pallas_call(
        functools.partial(attention_kernel, nope, width - nope, rank, value),
        grid=(steps,),
        in_specs=[
            pl.BlockSpec((span, lat), fixed),
            pl.BlockSpec((lat, span), fixed),
            pl.BlockSpec((span, tok), fixed),
            pl.BlockSpec((tok, PAIR * width), columns),
            pl.BlockSpec((tok, PAIR * value), columns),
            pl.BlockSpec((PAIR, nope, rank), weight),
            pl.BlockSpec((PAIR, value, rank), weight),
        ]
        + [pl.BlockSpec(memory_space=pl.ANY) for _ in filled],
        out_specs=[
            pl.BlockSpec((tok, PAIR * value), columns),
            pl.BlockSpec((tok, PAIR * width), columns),
            pl.BlockSpec((span, lat), fixed),
            pl.BlockSpec((PAIR, nope, rank), own),
            pl.BlockSpec((PAIR, value, rank), own),
        ],
        out_shape=[
            jax.ShapeDtypeStruct((tok, heads * value), jnp.bfloat16),
            jax.ShapeDtypeStruct((tok, heads * width), jnp.bfloat16),
            jax.ShapeDtypeStruct((span, lat), jnp.float32),
            jax.ShapeDtypeStruct((here, nope, rank), jnp.bfloat16),
            jax.ShapeDtypeStruct((here, value, rank), jnp.bfloat16),
        ],
        input_output_aliases={7 + i: i for i in range(len(filled))},
        compiler_params=pltpu.CompilerParams(vmem_limit_bytes=48 * 1024 * 1024),
        cost_estimate=pl.CostEstimate(
            flops=flops, bytes_accessed=8 * span * lat, transcendentals=tok * here * span
        ),
    )(keys, keys_t, bias, query, d_out, w_uk, w_uv, *filled)


def shifted(block, axis, distance):
    devices = range(lax.axis_size(axis))
    route = [(i - distance, i) for i in devices if i - distance in devices]
    return lax.ppermute(block, axis, route)


def mask_bias(tok, block_mask, segments):
    position = lax.axis_index("ctx")
    offsets = jnp.arange(tok, dtype=jnp.int32)
    seg_query = lax.dynamic_slice_in_dim(segments, position * tok, tok)
    parts = []
    for back in range(SPAN + 1):
        block = position - back
        clamped = jnp.maximum(block, 0)
        seg_key = lax.dynamic_slice_in_dim(segments, clamped * tok, tok)
        granted = block_mask[position, clamped] == 1
        allowed = (block >= 0) & ((seg_query[None, :] == seg_key[:, None]) | granted)
        if back == 0:
            allowed = allowed & (offsets[:, None] <= offsets[None, :])
        parts.append(jnp.where(allowed, 0.0, -jnp.inf).astype(jnp.float32))
    return jnp.concatenate(parts, axis=0)


def body(latent, query, d_out, w_uk, w_uv, block_mask, segments):
    tok = latent.shape[0]
    heads = w_uk.shape[0]
    chunks = CHUNKS
    bias = mask_bias(tok, block_mask, segments)
    keys = jnp.concatenate([latent] + [shifted(latent, "ctx", d) for d in range(1, SPAN + 1)], axis=0)
    keys_t = keys.T
    filled = ()
    d_keys = None
    uk_parts, uv_parts = [], []
    for chunk in range(chunks):
        att, dq, part, uk, uv = attend(
            chunk, chunks, keys, keys_t, bias, query, d_out, w_uk, w_uv, *filled
        )
        filled = (att, dq)
        d_keys = part if d_keys is None else d_keys + part
        if uk_parts:
            uk, uv, uk_parts[-1], uv_parts[-1] = lax.optimization_barrier(
                (uk, uv, uk_parts[-1], uv_parts[-1])
            )
        uk, uv = lax.psum((uk, uv), "ctx")
        uk_parts.append(uk)
        uv_parts.append(uv)
    d_keys = d_keys.astype(jnp.bfloat16).reshape(SPAN + 1, tok, -1)
    shares = lax.psum_scatter(d_keys, "head", scatter_dimension=1, tiled=True)
    total = shares[0].astype(jnp.float32)
    for back in range(1, SPAN + 1):
        total = total + shifted(shares[back], "ctx", -back).astype(jnp.float32)
    d_latent = lax.all_gather(total.astype(jnp.bfloat16), "head", axis=0, tiled=True)
    d_w_uk = jnp.concatenate(uk_parts, axis=0).astype(jnp.float32)
    d_w_uv = jnp.concatenate(uv_parts, axis=0).astype(jnp.float32)
    return att, dq, d_latent.astype(jnp.float32), d_w_uk, d_w_uv


def solution(mesh):
    in_specs = (
        P("ctx", None),
        P("ctx", "head"),
        P("ctx", "head"),
        P("head", None, None),
        P("head", None, None),
        P(),
        P(),
    )
    out_specs = (
        P("ctx", "head"),
        P("ctx", "head"),
        P("ctx", None),
        P("head", None, None),
        P("head", None, None),
    )
    return jax.shard_map(body, mesh=mesh, in_specs=in_specs, out_specs=out_specs, check_vma=False)
```

```python
import functools
import math

import jax
import jax.numpy as jnp
from jax import lax
from jax.experimental import pallas as pl
from jax.experimental.pallas import tpu as pltpu
from jax.sharding import PartitionSpec as P

SPAN = 2
PAIR = 2
LAGS = (1, 2, 4, 6)


def dot(a, b):
    return lax.dot_general(a, b, (((1,), (0,)), ((), ())), preferred_element_type=jnp.float32)


def dot_t(a, b):
    return lax.dot_general(a, b, (((1,), (1,)), ((), ())), preferred_element_type=jnp.float32)


def attention_kernel(
    nope, rope, rank, value, steps, n, peers,
    keys_ref, keys_t_ref, bias_ref, query_ref, grads_ref, uk_ref, uv_ref,
    att_ref, dq_ref, dlat_ref, duk_ref, duv_ref,
    dkeys, own, from_pair, mid, from_line, final, sent, from_head, shifts, from_ctx, gathered,
    pair_send, pair_recv, line_send, line_recv, back_send, back_recv, last_send, last_recv,
    head_send, head_recv, ctx_send, ctx_recv, out_send, out_recv,
):
    bf16, f32 = jnp.bfloat16, jnp.float32
    width = nope + rope
    inv_root = 1.0 / math.sqrt(width)
    to_log2 = inv_root * math.log2(math.e)
    step = pl.program_id(0)
    me = lax.axis_index("ctx")
    head_me = lax.axis_index("head")
    parity = lax.rem(me, 2)
    place = me // 2
    line = n // 2
    half = own.shape[1] // 2
    part = half // line
    tok = att_ref.shape[0]
    quarter = tok // peers

    def remote(src, dst, send, recv, target):
        return pltpu.make_async_remote_copy(
            src_ref=src, dst_ref=dst, send_sem=send, recv_sem=recv,
            device_id=target, device_id_type=pl.DeviceIdType.MESH,
        )

    def half_rows(which):
        return pl.ds(pl.multiple_of(which * half, 16), half)

    def part_rows(at):
        return pl.ds(pl.multiple_of(at * part, 16), part)

    def pair_copy(c):
        return remote(
            own.at[c, half_rows(1 - parity)], from_pair.at[c],
            pair_send.at[c], pair_recv.at[c], {"ctx": me + 1 - 2 * parity},
        )

    def line_copy(c, d):
        peer = lax.rem(place + d, line)
        return remote(
            mid.at[c, part_rows(peer)], from_line.at[c, d - 1],
            line_send.at[c, d - 1], line_recv.at[c, d - 1], {"ctx": peer * 2 + parity},
        )

    def back_copy(c, d):
        peer = lax.rem(place + d, line)
        rows = pl.ds(pl.multiple_of(parity * half + place * part, 16), part)
        return remote(
            final.at[c, rows], final.at[c, rows],
            back_send.at[c, d - 1], back_recv.at[c, d - 1], {"ctx": peer * 2 + parity},
        )

    def last_copy(c):
        rows = half_rows(parity)
        return remote(
            final.at[c, rows], final.at[c, rows],
            last_send.at[c], last_recv.at[c], {"ctx": me + 1 - 2 * parity},
        )

    def head_copy(d):
        peer = lax.rem(head_me + d, peers)
        rows = pl.ds(pl.multiple_of(peer * quarter, 16), quarter)
        return remote(
            sent.at[:, rows, :], from_head.at[d - 1],
            head_send.at[d - 1], head_recv.at[d - 1], {"head": peer},
        )

    def ctx_copy(d):
        return remote(
            shifts.at[d - 1], from_ctx.at[d - 1],
            ctx_send.at[d - 1], ctx_recv.at[d - 1], {"ctx": lax.rem(me - d + n, n)},
        )

    def out_copy(d):
        peer = lax.rem(head_me + d, peers)
        rows = pl.ds(pl.multiple_of(head_me * quarter, 16), quarter)
        return remote(
            gathered.at[rows], gathered.at[rows],
            out_send.at[d - 1], out_recv.at[d - 1], {"head": peer},
        )

    @pl.when(step == 0)
    def _():
        dkeys[...] = jnp.zeros_like(dkeys)
        barrier = pltpu.get_barrier_semaphore()
        for d in range(1, n):
            pl.semaphore_signal(
                barrier, inc=1, device_id={"ctx": lax.rem(me + d, n)},
                device_id_type=pl.DeviceIdType.MESH,
            )
        for d in range(1, peers):
            pl.semaphore_signal(
                barrier, inc=1, device_id={"head": lax.rem(head_me + d, peers)},
                device_id_type=pl.DeviceIdType.MESH,
            )
        pl.semaphore_wait(barrier, n - 1 + peers - 1)

    @pl.when(step < steps)
    def _():
        queries = query_ref[...]
        for head in range(PAIR):
            q_nope = queries[:, head * width : head * width + nope]
            q_rope = queries[:, head * width + nope : (head + 1) * width]
            grads = grads_ref[:, head * value : (head + 1) * value]
            w_uk = uk_ref[head]
            w_uv = uv_ref[head]
            base = head * (nope + value)
            absorbed = dot(q_nope, w_uk).astype(bf16)
            d_out_latent = dot(grads, w_uv).astype(bf16)
            content = keys_ref[:, :rank]
            scores = dot_t(content, absorbed) + dot_t(keys_ref[:, rank:], q_rope)
            scores = scores * to_log2 + bias_ref[...]
            weights = jnp.exp2(scores - jnp.max(scores, axis=0, keepdims=True))
            probs = weights * (1.0 / jnp.sum(weights, axis=0, keepdims=True))
            low = probs.astype(bf16)
            out_t = dot(keys_t_ref[:rank, :], low).astype(bf16)
            att_t = dot(w_uv, out_t)
            att_ref[:, head * value : (head + 1) * value] = att_t.T.astype(bf16)
            own[step, base + nope : base + nope + value] = dot_t(grads.T, out_t).astype(bf16)
            d_probs = dot_t(content, d_out_latent)
            delta = jnp.sum(probs * d_probs, axis=0, keepdims=True)
            d_scores = (probs * (d_probs - delta) * inv_root).astype(bf16)
            d_full_t = dot(keys_t_ref[...], d_scores)
            d_absorbed_t = d_full_t[:rank].astype(bf16)
            d_nope_t = dot(w_uk, d_absorbed_t)
            dq_ref[:, head * width : (head + 1) * width] = jnp.concatenate(
                [d_nope_t, d_full_t[rank:]], axis=0
            ).T.astype(bf16)
            own[step, base : base + nope] = dot_t(q_nope.T, d_absorbed_t).astype(bf16)
            dkeys[:, :rank] += dot(d_scores, absorbed) + dot(low, d_out_latent)
            dkeys[:, rank:] += dot(d_scores, q_rope)
        pair_copy(step).start()

    @pl.when(step == steps - 1)
    def _():
        for back in range(SPAN + 1):
            sent[back] = dkeys[back * tok : (back + 1) * tok, :].astype(bf16)
        for d in range(1, peers):
            head_copy(d).start()

    at1 = step - LAGS[0]

    @pl.when((at1 >= 0) & (at1 < steps))
    def _():
        pair_copy(at1).wait()
        mine = own[at1, half_rows(parity)].astype(f32)
        mid[at1] = (mine + from_pair[at1].astype(f32)).astype(bf16)
        for d in range(1, line):
            line_copy(at1, d).start()

    at2 = step - LAGS[1]

    @pl.when((at2 >= 0) & (at2 < steps))
    def _():
        total = mid[at2, part_rows(place)].astype(f32)
        for d in range(1, line):
            line_copy(at2, d).wait()
            total = total + from_line[at2, d - 1].astype(f32)
        rows = pl.ds(pl.multiple_of(parity * half + place * part, 16), part)
        final[at2, rows] = total.astype(bf16)
        for d in range(1, line):
            back_copy(at2, d).start()

    at3 = step - LAGS[2]

    @pl.when((at3 >= 0) & (at3 < steps))
    def _():
        for d in range(1, line):
            back_copy(at3, d).wait()
        last_copy(at3).start()

    at4 = step - LAGS[3]

    @pl.when((at4 >= 0) & (at4 < steps))
    def _():
        last_copy(at4).wait()
        for head in range(PAIR):
            base = head * (nope + value)
            duk_ref[head] = final[at4, base : base + nope]
            duv_ref[head] = final[at4, base + nope : base + nope + value]

    own_rows = pl.ds(pl.multiple_of(head_me * quarter, 16), quarter)

    @pl.when(step == steps)
    def _():
        for d in range(1, peers):
            head_copy(d).wait()
        for back in range(1, SPAN + 1):
            block = sent[back, own_rows, :].astype(f32)
            for d in range(1, peers):
                block = block + from_head[d - 1, back].astype(f32)
            shifts[back - 1] = block.astype(bf16)

            @pl.when(me >= back)
            def _():
                ctx_copy(back).start()

        from_ctx_zero = jnp.zeros_like(from_ctx[0])
        for back in range(1, SPAN + 1):

            @pl.when(me + back >= n)
            def _():
                from_ctx[back - 1] = from_ctx_zero

    @pl.when(step == steps + 1)
    def _():
        block = sent[0, own_rows, :].astype(f32)
        for d in range(1, peers):
            block = block + from_head[d - 1, 0].astype(f32)
        for back in range(1, SPAN + 1):

            @pl.when(me >= back)
            def _():
                ctx_copy(back).wait_send()

            @pl.when(me + back < n)
            def _():
                ctx_copy(back).wait_recv()

            block = block + from_ctx[back - 1].astype(f32)
        gathered[own_rows] = block.astype(bf16)
        for d in range(1, peers):
            out_copy(d).start()

    @pl.when(step == steps + 3)
    def _():
        for d in range(1, peers):
            out_copy(d).wait()
        dlat_ref[...] = gathered[...]


def attend(n, peers, keys, keys_t, bias, query, d_out, w_uk, w_uv):
    tok = query.shape[0]
    heads, nope, rank = w_uk.shape
    value = w_uv.shape[1]
    width = query.shape[1] // heads
    span, lat = keys.shape
    steps = heads // PAIR
    rows = PAIR * (nope + value)
    half = rows // 2
    line = n // 2
    part = half // line
    quarter = tok // peers
    bf16 = jnp.bfloat16
    fixed = lambda i: (0, 0)
    columns = lambda i: (0, jnp.minimum(i, steps - 1))
    weight = lambda i: (jnp.minimum(i, steps - 1), 0, 0)
    late = lambda i: (jnp.maximum(i - LAGS[3], 0), 0, 0)
    flops = 2 * tok * heads * (span * (3 * lat + 3 * rank) + 6 * nope * rank)
    sem = pltpu.SemaphoreType.DMA
    return pl.pallas_call(
        functools.partial(
            attention_kernel, nope, width - nope, rank, value, steps, n, peers
        ),
        grid=(steps + LAGS[3],),
        in_specs=[
            pl.BlockSpec((span, lat), fixed),
            pl.BlockSpec((lat, span), fixed),
            pl.BlockSpec((span, tok), fixed),
            pl.BlockSpec((tok, PAIR * width), columns),
            pl.BlockSpec((tok, PAIR * value), columns),
            pl.BlockSpec((PAIR, nope, rank), weight),
            pl.BlockSpec((PAIR, value, rank), weight),
        ],
        out_specs=[
            pl.BlockSpec((tok, PAIR * value), columns),
            pl.BlockSpec((tok, PAIR * width), columns),
            pl.BlockSpec((tok, lat), fixed),
            pl.BlockSpec((PAIR, nope, rank), late),
            pl.BlockSpec((PAIR, value, rank), late),
        ],
        out_shape=[
            jax.ShapeDtypeStruct((tok, heads * value), bf16),
            jax.ShapeDtypeStruct((tok, heads * width), bf16),
            jax.ShapeDtypeStruct((tok, lat), bf16),
            jax.ShapeDtypeStruct((heads, nope, rank), bf16),
            jax.ShapeDtypeStruct((heads, value, rank), bf16),
        ],
        scratch_shapes=[
            pltpu.VMEM((span, lat), jnp.float32),
            pltpu.VMEM((steps, rows, rank), bf16),
            pltpu.VMEM((steps, half, rank), bf16),
            pltpu.VMEM((steps, half, rank), bf16),
            pltpu.VMEM((steps, line - 1, part, rank), bf16),
            pltpu.VMEM((steps, rows, rank), bf16),
            pltpu.VMEM((SPAN + 1, tok, lat), bf16),
            pltpu.VMEM((peers - 1, SPAN + 1, quarter, lat), bf16),
            pltpu.VMEM((SPAN, quarter, lat), bf16),
            pltpu.VMEM((SPAN, quarter, lat), bf16),
            pltpu.VMEM((tok, lat), bf16),
            sem((steps,)), sem((steps,)),
            sem((steps, line - 1)), sem((steps, line - 1)),
            sem((steps, line - 1)), sem((steps, line - 1)),
            sem((steps,)), sem((steps,)),
            sem((peers - 1,)), sem((peers - 1,)),
            sem((SPAN,)), sem((SPAN,)),
            sem((peers - 1,)), sem((peers - 1,)),
        ],
        compiler_params=pltpu.CompilerParams(
            vmem_limit_bytes=52 * 1024 * 1024, collective_id=0, has_side_effects=True
        ),
        cost_estimate=pl.CostEstimate(
            flops=flops, bytes_accessed=16 * span * lat, transcendentals=tok * heads * span
        ),
    )(keys, keys_t, bias, query, d_out, w_uk, w_uv)


def shifted(block, axis, distance):
    devices = range(lax.axis_size(axis))
    route = [(i - distance, i) for i in devices if i - distance in devices]
    return lax.ppermute(block, axis, route)


def mask_bias(tok, block_mask, segments):
    position = lax.axis_index("ctx")
    offsets = jnp.arange(tok, dtype=jnp.int32)
    seg_query = lax.dynamic_slice_in_dim(segments, position * tok, tok)
    parts = []
    for back in range(SPAN + 1):
        block = position - back
        clamped = jnp.maximum(block, 0)
        seg_key = lax.dynamic_slice_in_dim(segments, clamped * tok, tok)
        granted = block_mask[position, clamped] == 1
        allowed = (block >= 0) & ((seg_query[None, :] == seg_key[:, None]) | granted)
        if back == 0:
            allowed = allowed & (offsets[:, None] <= offsets[None, :])
        parts.append(jnp.where(allowed, 0.0, -jnp.inf).astype(jnp.float32))
    return jnp.concatenate(parts, axis=0)


def body(latent, query, d_out, w_uk, w_uv, block_mask, segments):
    tok = latent.shape[0]
    bias = mask_bias(tok, block_mask, segments)
    keys = jnp.concatenate([latent] + [shifted(latent, "ctx", d) for d in range(1, SPAN + 1)], axis=0)
    att, dq, d_latent, d_w_uk, d_w_uv = attend(
        lax.axis_size("ctx"), lax.axis_size("head"), keys, keys.T, bias, query, d_out, w_uk, w_uv
    )
    wide = jnp.float32
    return att, dq, d_latent.astype(wide), d_w_uk.astype(wide), d_w_uv.astype(wide)


def solution(mesh):
    in_specs = (
        P("ctx", None),
        P("ctx", "head"),
        P("ctx", "head"),
        P("head", None, None),
        P("head", None, None),
        P(),
        P(),
    )
    out_specs = (
        P("ctx", "head"),
        P("ctx", "head"),
        P("ctx", None),
        P("head", None, None),
        P("head", None, None),
    )
    return jax.shard_map(body, mesh=mesh, in_specs=in_specs, out_specs=out_specs, check_vma=False)
```

```python
import functools
import math

import jax
import jax.numpy as jnp
from jax import lax
from jax.experimental import pallas as pl
from jax.experimental.pallas import tpu as pltpu
from jax.sharding import PartitionSpec as P

SPAN = 2
PAIR = 2
LAGS = (1, 3, 6, 8)


def dot(a, b):
    return lax.dot_general(a, b, (((1,), (0,)), ((), ())), preferred_element_type=jnp.float32)


def dot_t(a, b):
    return lax.dot_general(a, b, (((1,), (1,)), ((), ())), preferred_element_type=jnp.float32)


def attention_kernel(
    nope, rope, rank, value, steps, n, peers,
    lat_t_ref, bias_ref, query_ref, grads_ref, uk_ref, uv_ref,
    att_ref, dq_ref, dlat_ref, duk_ref, duv_ref,
    keys_ref, keys_t_ref, dkeys, own, from_pair, mid, from_line, final, sent, from_head, shifts, from_ctx, gathered,
    pair_send, pair_recv, line_send, line_recv, back_send, back_recv, last_send, last_recv,
    head_send, head_recv, ctx_send, ctx_recv, out_send, out_recv, key_send, key_recv,
):
    bf16, f32 = jnp.bfloat16, jnp.float32
    width = nope + rope
    inv_root = 1.0 / math.sqrt(width)
    to_log2 = inv_root * math.log2(math.e)
    step = pl.program_id(0)
    me = lax.axis_index("ctx")
    head_me = lax.axis_index("head")
    parity = lax.rem(me, 2)
    place = me // 2
    line = n // 2
    half = own.shape[1] // 2
    part = half // line
    tok = att_ref.shape[0]
    quarter = tok // peers

    def remote(src, dst, send, recv, target):
        return pltpu.make_async_remote_copy(
            src_ref=src, dst_ref=dst, send_sem=send, recv_sem=recv,
            device_id=target, device_id_type=pl.DeviceIdType.MESH,
        )

    def half_rows(which):
        return pl.ds(pl.multiple_of(which * half, 16), half)

    def part_rows(at):
        return pl.ds(pl.multiple_of(at * part, 16), part)

    def pair_copy(c):
        return remote(
            own.at[c, half_rows(1 - parity)], from_pair.at[c],
            pair_send.at[c], pair_recv.at[c], {"ctx": me + 1 - 2 * parity},
        )

    def line_copy(c, d):
        peer = lax.rem(place + d, line)
        return remote(
            mid.at[c, part_rows(peer)], from_line.at[c, d - 1],
            line_send.at[c, d - 1], line_recv.at[c, d - 1], {"ctx": peer * 2 + parity},
        )

    def back_copy(c, d):
        peer = lax.rem(place + d, line)
        rows = pl.ds(pl.multiple_of(parity * half + place * part, 16), part)
        return remote(
            final.at[c, rows], final.at[c, rows],
            back_send.at[c, d - 1], back_recv.at[c, d - 1], {"ctx": peer * 2 + parity},
        )

    def last_copy(c):
        rows = half_rows(parity)
        return remote(
            final.at[c, rows], final.at[c, rows],
            last_send.at[c], last_recv.at[c], {"ctx": me + 1 - 2 * parity},
        )

    def head_copy(d):
        peer = lax.rem(head_me + d, peers)
        rows = pl.ds(pl.multiple_of(peer * quarter, 16), quarter)
        return remote(
            sent.at[:, rows, :], from_head.at[d - 1],
            head_send.at[d - 1], head_recv.at[d - 1], {"head": peer},
        )

    def ctx_copy(d):
        return remote(
            shifts.at[d - 1], from_ctx.at[d - 1],
            ctx_send.at[d - 1], ctx_recv.at[d - 1], {"ctx": lax.rem(me - d + n, n)},
        )

    def out_copy(d):
        peer = lax.rem(head_me + d, peers)
        rows = pl.ds(pl.multiple_of(head_me * quarter, 16), quarter)
        return remote(
            gathered.at[rows], gathered.at[rows],
            out_send.at[d - 1], out_recv.at[d - 1], {"head": peer},
        )

    def key_copy(d):
        return remote(
            keys_t_ref.at[:, :tok], keys_t_ref.at[:, d * tok : (d + 1) * tok],
            key_send.at[d - 1], key_recv.at[d - 1], {"ctx": lax.rem(me + d, n)},
        )

    @pl.when(step == 0)
    def _():
        barrier = pltpu.get_barrier_semaphore()
        for d in range(1, n):
            pl.semaphore_signal(
                barrier, inc=1, device_id={"ctx": lax.rem(me + d, n)},
                device_id_type=pl.DeviceIdType.MESH,
            )
        for d in range(1, peers):
            pl.semaphore_signal(
                barrier, inc=1, device_id={"head": lax.rem(head_me + d, peers)},
                device_id_type=pl.DeviceIdType.MESH,
            )
        keys_t_ref[:, :tok] = lat_t_ref[...]
        pl.semaphore_wait(barrier, n - 1 + peers - 1)
        for d in range(1, SPAN + 1):

            @pl.when(me + d < n)
            def _():
                key_copy(d).start()

            @pl.when(me < d)
            def _():
                keys_t_ref[:, d * tok : (d + 1) * tok] = jnp.zeros(
                    (keys_t_ref.shape[0], tok), keys_t_ref.dtype
                )

        dkeys[...] = jnp.zeros_like(dkeys)
        keys_ref[:tok, :] = lat_t_ref[...].T
        for d in range(1, SPAN + 1):

            @pl.when(me >= d)
            def _():
                key_copy(d).wait_recv()

            keys_ref[d * tok : (d + 1) * tok, :] = keys_t_ref[:, d * tok : (d + 1) * tok].T
        for d in range(1, SPAN + 1):

            @pl.when(me + d < n)
            def _():
                key_copy(d).wait_send()

    @pl.when(step < steps)
    def _():
        queries = query_ref[...]
        for head in range(PAIR):
            q_nope = queries[:, head * width : head * width + nope]
            q_rope = queries[:, head * width + nope : (head + 1) * width]
            grads = grads_ref[:, head * value : (head + 1) * value]
            w_uk = uk_ref[head]
            w_uv = uv_ref[head]
            base = head * (nope + value)
            absorbed = dot(q_nope, w_uk).astype(bf16)
            d_out_latent = dot(grads, w_uv).astype(bf16)
            content = keys_ref[:, :rank]
            scores = dot_t(content, absorbed) + dot_t(keys_ref[:, rank:], q_rope)
            scores = scores * to_log2 + bias_ref[...]
            weights = jnp.exp2(scores - jnp.max(scores, axis=0, keepdims=True))
            probs = weights * (1.0 / jnp.sum(weights, axis=0, keepdims=True))
            low = probs.astype(bf16)
            out_t = dot(keys_t_ref[:rank, :], low).astype(bf16)
            att_t = dot(w_uv, out_t)
            att_ref[:, head * value : (head + 1) * value] = att_t.T.astype(bf16)
            own[step, base + nope : base + nope + value] = dot_t(grads.T, out_t).astype(bf16)
            d_probs = dot_t(content, d_out_latent)
            delta = jnp.sum(probs * d_probs, axis=0, keepdims=True)
            d_scores = (probs * (d_probs - delta) * inv_root).astype(bf16)
            d_full_t = dot(keys_t_ref[...], d_scores)
            d_absorbed_t = d_full_t[:rank].astype(bf16)
            d_nope_t = dot(w_uk, d_absorbed_t)
            dq_ref[:, head * width : (head + 1) * width] = jnp.concatenate(
                [d_nope_t, d_full_t[rank:]], axis=0
            ).T.astype(bf16)
            own[step, base : base + nope] = dot_t(q_nope.T, d_absorbed_t).astype(bf16)
            dkeys[:, :rank] += dot(d_scores, absorbed) + dot(low, d_out_latent)
            dkeys[:, rank:] += dot(d_scores, q_rope)
        pair_copy(step).start()

    @pl.when(step == steps - 1)
    def _():
        for back in range(SPAN + 1):
            sent[back] = dkeys[back * tok : (back + 1) * tok, :].astype(bf16)
        for d in range(1, peers):
            head_copy(d).start()

    at1 = step - LAGS[0]

    @pl.when((at1 >= 0) & (at1 < steps))
    def _():
        pair_copy(at1).wait()
        mine = own[at1, half_rows(parity)].astype(f32)
        mid[at1] = (mine + from_pair[at1].astype(f32)).astype(bf16)
        for d in range(1, line):
            line_copy(at1, d).start()

    at2 = step - LAGS[1]

    @pl.when((at2 >= 0) & (at2 < steps))
    def _():
        total = mid[at2, part_rows(place)].astype(f32)
        for d in range(1, line):
            line_copy(at2, d).wait()
            total = total + from_line[at2, d - 1].astype(f32)
        rows = pl.ds(pl.multiple_of(parity * half + place * part, 16), part)
        final[at2, rows] = total.astype(bf16)
        for d in range(1, line):
            back_copy(at2, d).start()

    at3 = step - LAGS[2]

    @pl.when((at3 >= 0) & (at3 < steps))
    def _():
        for d in range(1, line):
            back_copy(at3, d).wait()
        last_copy(at3).start()

    at4 = step - LAGS[3]

    @pl.when((at4 >= 0) & (at4 < steps))
    def _():
        last_copy(at4).wait()
        for head in range(PAIR):
            base = head * (nope + value)
            duk_ref[head] = final[at4, base : base + nope]
            duv_ref[head] = final[at4, base + nope : base + nope + value]

    own_rows = pl.ds(pl.multiple_of(head_me * quarter, 16), quarter)

    @pl.when(step == steps)
    def _():
        for d in range(1, peers):
            head_copy(d).wait()
        for back in range(1, SPAN + 1):
            block = sent[back, own_rows, :].astype(f32)
            for d in range(1, peers):
                block = block + from_head[d - 1, back].astype(f32)
            shifts[back - 1] = block.astype(bf16)

            @pl.when(me >= back)
            def _():
                ctx_copy(back).start()

        from_ctx_zero = jnp.zeros_like(from_ctx[0])
        for back in range(1, SPAN + 1):

            @pl.when(me + back >= n)
            def _():
                from_ctx[back - 1] = from_ctx_zero

    @pl.when(step == steps + 1)
    def _():
        block = sent[0, own_rows, :].astype(f32)
        for d in range(1, peers):
            block = block + from_head[d - 1, 0].astype(f32)
        for back in range(1, SPAN + 1):

            @pl.when(me >= back)
            def _():
                ctx_copy(back).wait_send()

            @pl.when(me + back < n)
            def _():
                ctx_copy(back).wait_recv()

            block = block + from_ctx[back - 1].astype(f32)
        gathered[own_rows] = block.astype(bf16)
        for d in range(1, peers):
            out_copy(d).start()

    @pl.when(step == steps + 3)
    def _():
        for d in range(1, peers):
            out_copy(d).wait()
        dlat_ref[...] = gathered[...]


def attend(n, peers, lat_t, bias, query, d_out, w_uk, w_uv):
    tok = query.shape[0]
    heads, nope, rank = w_uk.shape
    value = w_uv.shape[1]
    width = query.shape[1] // heads
    lat = lat_t.shape[0]
    span = bias.shape[0]
    steps = heads // PAIR
    rows = PAIR * (nope + value)
    half = rows // 2
    line = n // 2
    part = half // line
    quarter = tok // peers
    bf16 = jnp.bfloat16
    fixed = lambda i: (0, 0)
    columns = lambda i: (0, jnp.minimum(i, steps - 1))
    weight = lambda i: (jnp.minimum(i, steps - 1), 0, 0)
    late = lambda i: (jnp.maximum(i - LAGS[3], 0), 0, 0)
    flops = 2 * tok * heads * (span * (3 * lat + 3 * rank) + 6 * nope * rank)
    sem = pltpu.SemaphoreType.DMA
    return pl.pallas_call(
        functools.partial(
            attention_kernel, nope, width - nope, rank, value, steps, n, peers
        ),
        grid=(steps + LAGS[3],),
        in_specs=[
            pl.BlockSpec((lat, tok), fixed),
            pl.BlockSpec((span, tok), fixed),
            pl.BlockSpec((tok, PAIR * width), columns),
            pl.BlockSpec((tok, PAIR * value), columns),
            pl.BlockSpec((PAIR, nope, rank), weight),
            pl.BlockSpec((PAIR, value, rank), weight),
        ],
        out_specs=[
            pl.BlockSpec((tok, PAIR * value), columns),
            pl.BlockSpec((tok, PAIR * width), columns),
            pl.BlockSpec((tok, lat), fixed),
            pl.BlockSpec((PAIR, nope, rank), late),
            pl.BlockSpec((PAIR, value, rank), late),
        ],
        out_shape=[
            jax.ShapeDtypeStruct((tok, heads * value), bf16),
            jax.ShapeDtypeStruct((tok, heads * width), bf16),
            jax.ShapeDtypeStruct((tok, lat), bf16),
            jax.ShapeDtypeStruct((heads, nope, rank), bf16),
            jax.ShapeDtypeStruct((heads, value, rank), bf16),
        ],
        scratch_shapes=[
            pltpu.VMEM((span, lat), bf16),
            pltpu.VMEM((lat, span), bf16),
            pltpu.VMEM((span, lat), jnp.float32),
            pltpu.VMEM((steps, rows, rank), bf16),
            pltpu.VMEM((steps, half, rank), bf16),
            pltpu.VMEM((steps, half, rank), bf16),
            pltpu.VMEM((steps, line - 1, part, rank), bf16),
            pltpu.VMEM((steps, rows, rank), bf16),
            pltpu.VMEM((SPAN + 1, tok, lat), bf16),
            pltpu.VMEM((peers - 1, SPAN + 1, quarter, lat), bf16),
            pltpu.VMEM((SPAN, quarter, lat), bf16),
            pltpu.VMEM((SPAN, quarter, lat), bf16),
            pltpu.VMEM((tok, lat), bf16),
            sem((steps,)), sem((steps,)),
            sem((steps, line - 1)), sem((steps, line - 1)),
            sem((steps, line - 1)), sem((steps, line - 1)),
            sem((steps,)), sem((steps,)),
            sem((peers - 1,)), sem((peers - 1,)),
            sem((SPAN,)), sem((SPAN,)),
            sem((peers - 1,)), sem((peers - 1,)),
            sem((SPAN,)), sem((SPAN,)),
        ],
        compiler_params=pltpu.CompilerParams(
            vmem_limit_bytes=52 * 1024 * 1024, collective_id=0, has_side_effects=True
        ),
        cost_estimate=pl.CostEstimate(
            flops=flops, bytes_accessed=16 * span * lat, transcendentals=tok * heads * span
        ),
    )(lat_t, bias, query, d_out, w_uk, w_uv)


def mask_bias(tok, block_mask, segments):
    position = lax.axis_index("ctx")
    offsets = jnp.arange(tok, dtype=jnp.int32)
    seg_query = lax.dynamic_slice_in_dim(segments, position * tok, tok)
    parts = []
    for back in range(SPAN + 1):
        block = position - back
        clamped = jnp.maximum(block, 0)
        seg_key = lax.dynamic_slice_in_dim(segments, clamped * tok, tok)
        granted = block_mask[position, clamped] == 1
        allowed = (block >= 0) & ((seg_query[None, :] == seg_key[:, None]) | granted)
        if back == 0:
            allowed = allowed & (offsets[:, None] <= offsets[None, :])
        parts.append(jnp.where(allowed, 0.0, -jnp.inf).astype(jnp.float32))
    return jnp.concatenate(parts, axis=0)


def body(latent, query, d_out, w_uk, w_uv, block_mask, segments):
    tok = latent.shape[0]
    bias = mask_bias(tok, block_mask, segments)
    att, dq, d_latent, d_w_uk, d_w_uv = attend(
        lax.axis_size("ctx"), lax.axis_size("head"), latent.T, bias, query, d_out, w_uk, w_uv
    )
    wide = jnp.float32
    return att, dq, d_latent.astype(wide), d_w_uk.astype(wide), d_w_uv.astype(wide)


def solution(mesh):
    in_specs = (
        P("ctx", None),
        P("ctx", "head"),
        P("ctx", "head"),
        P("head", None, None),
        P("head", None, None),
        P(),
        P(),
    )
    out_specs = (
        P("ctx", "head"),
        P("ctx", "head"),
        P("ctx", None),
        P("head", None, None),
        P("head", None, None),
    )
    return jax.shard_map(body, mesh=mesh, in_specs=in_specs, out_specs=out_specs, check_vma=False)
```

```python
import functools
import math

import jax
import jax.numpy as jnp
from jax import lax
from jax.experimental import pallas as pl
from jax.experimental.pallas import tpu as pltpu
from jax.sharding import PartitionSpec as P

SPAN = 2
PAIR = 2
LAGS = (1, 2, 4, 6)


def dot(a, b):
    return lax.dot_general(a, b, (((1,), (0,)), ((), ())), preferred_element_type=jnp.float32)


def dot_t(a, b):
    return lax.dot_general(a, b, (((1,), (1,)), ((), ())), preferred_element_type=jnp.float32)


def attention_kernel(
    nope, rope, rank, value, steps, n, peers,
    lat_t_ref, bias_ref, query_ref, grads_ref, uk_ref, uv_ref,
    att_ref, dq_ref, dlat_ref, duk_ref, duv_ref,
    keys_ref, keys_t_ref, dkeys, own, from_pair, mid, from_line, final, sent, from_head, shifts, from_ctx, gathered,
    pair_send, pair_recv, line_send, line_recv, back_send, back_recv, last_send, last_recv,
    head_send, head_recv, ctx_send, ctx_recv, out_send, out_recv, key_send, key_recv,
    share_send, share_recv,
):
    bf16, f32 = jnp.bfloat16, jnp.float32
    width = nope + rope
    inv_root = 1.0 / math.sqrt(width)
    to_log2 = inv_root * math.log2(math.e)
    step = pl.program_id(0)
    me = lax.axis_index("ctx")
    head_me = lax.axis_index("head")
    parity = lax.rem(me, 2)
    place = me // 2
    line = n // 2
    half = own.shape[1] // 2
    part = half // line
    tok = att_ref.shape[0]
    quarter = tok // peers

    def remote(src, dst, send, recv, target):
        return pltpu.make_async_remote_copy(
            src_ref=src, dst_ref=dst, send_sem=send, recv_sem=recv,
            device_id=target, device_id_type=pl.DeviceIdType.MESH,
        )

    def half_rows(which):
        return pl.ds(pl.multiple_of(which * half, 16), half)

    def part_rows(at):
        return pl.ds(pl.multiple_of(at * part, 16), part)

    def pair_copy(c):
        return remote(
            own.at[c, half_rows(1 - parity)], from_pair.at[c],
            pair_send.at[c], pair_recv.at[c], {"ctx": me + 1 - 2 * parity},
        )

    def line_copy(c, d):
        peer = lax.rem(place + d, line)
        return remote(
            mid.at[c, part_rows(peer)], from_line.at[c, d - 1],
            line_send.at[c, d - 1], line_recv.at[c, d - 1], {"ctx": peer * 2 + parity},
        )

    def back_copy(c, d):
        peer = lax.rem(place + d, line)
        rows = pl.ds(pl.multiple_of(parity * half + place * part, 16), part)
        return remote(
            final.at[c, rows], final.at[c, rows],
            back_send.at[c, d - 1], back_recv.at[c, d - 1], {"ctx": peer * 2 + parity},
        )

    def last_copy(c):
        rows = half_rows(parity)
        return remote(
            final.at[c, rows], final.at[c, rows],
            last_send.at[c], last_recv.at[c], {"ctx": me + 1 - 2 * parity},
        )

    def head_copy(d):
        peer = lax.rem(head_me + d, peers)
        rows = pl.ds(pl.multiple_of(peer * quarter, 16), quarter)
        return remote(
            sent.at[:, rows, :], from_head.at[d - 1],
            head_send.at[d - 1], head_recv.at[d - 1], {"head": peer},
        )

    def ctx_copy(d):
        return remote(
            shifts.at[d - 1], from_ctx.at[d - 1],
            ctx_send.at[d - 1], ctx_recv.at[d - 1], {"ctx": lax.rem(me - d + n, n)},
        )

    def out_copy(d):
        peer = lax.rem(head_me + d, peers)
        rows = pl.ds(pl.multiple_of(head_me * quarter, 16), quarter)
        return remote(
            gathered.at[rows], gathered.at[rows],
            out_send.at[d - 1], out_recv.at[d - 1], {"head": peer},
        )

    core = lax.rem(head_me, 2)
    core_half = keys_t_ref.shape[0] // 2
    core_rows = pl.ds(pl.multiple_of(core * core_half, 16), core_half)

    def key_copy(d):
        return remote(
            keys_t_ref.at[core_rows, :tok], keys_t_ref.at[core_rows, d * tok : (d + 1) * tok],
            key_send.at[d - 1], key_recv.at[d - 1], {"ctx": lax.rem(me + d, n)},
        )

    def share_copy(d):
        block = keys_t_ref.at[core_rows, d * tok : (d + 1) * tok]
        return remote(
            block, block, share_send.at[d - 1], share_recv.at[d - 1],
            {"head": head_me + 1 - 2 * core},
        )

    @pl.when(step == 0)
    def _():
        barrier = pltpu.get_barrier_semaphore()
        for d in range(1, n):
            pl.semaphore_signal(
                barrier, inc=1, device_id={"ctx": lax.rem(me + d, n)},
                device_id_type=pl.DeviceIdType.MESH,
            )
        for d in range(1, peers):
            pl.semaphore_signal(
                barrier, inc=1, device_id={"head": lax.rem(head_me + d, peers)},
                device_id_type=pl.DeviceIdType.MESH,
            )
        keys_t_ref[:, :tok] = lat_t_ref[...]
        pl.semaphore_wait(barrier, n - 1 + peers - 1)
        for d in range(1, SPAN + 1):

            @pl.when(me + d < n)
            def _():
                key_copy(d).start()

            @pl.when(me < d)
            def _():
                keys_t_ref[:, d * tok : (d + 1) * tok] = jnp.zeros(
                    (keys_t_ref.shape[0], tok), keys_t_ref.dtype
                )

        dkeys[...] = jnp.zeros_like(dkeys)
        keys_ref[:tok, :] = lat_t_ref[...].T
        for d in range(1, SPAN + 1):

            @pl.when(me >= d)
            def _():
                key_copy(d).wait_recv()
                share_copy(d).start()

        for d in range(1, SPAN + 1):

            @pl.when(me >= d)
            def _():
                share_copy(d).wait()

            keys_ref[d * tok : (d + 1) * tok, :] = keys_t_ref[:, d * tok : (d + 1) * tok].T
        for d in range(1, SPAN + 1):

            @pl.when(me + d < n)
            def _():
                key_copy(d).wait_send()

    @pl.when(step < steps)
    def _():
        queries = query_ref[...]
        for head in range(PAIR):
            q_nope = queries[:, head * width : head * width + nope]
            q_rope = queries[:, head * width + nope : (head + 1) * width]
            grads = grads_ref[:, head * value : (head + 1) * value]
            w_uk = uk_ref[head]
            w_uv = uv_ref[head]
            base = head * (nope + value)
            absorbed = dot(q_nope, w_uk).astype(bf16)
            d_out_latent = dot(grads, w_uv).astype(bf16)
            content = keys_ref[:, :rank]
            scores = dot_t(content, absorbed) + dot_t(keys_ref[:, rank:], q_rope)
            scores = scores * to_log2 + bias_ref[...]
            weights = jnp.exp2(scores - jnp.max(scores, axis=0, keepdims=True))
            probs = weights * (1.0 / jnp.sum(weights, axis=0, keepdims=True))
            low = probs.astype(bf16)
            out_t = dot(keys_t_ref[:rank, :], low).astype(bf16)
            att_t = dot(w_uv, out_t)
            att_ref[:, head * value : (head + 1) * value] = att_t.T.astype(bf16)
            own[step, base + nope : base + nope + value] = dot_t(grads.T, out_t).astype(bf16)
            d_probs = dot_t(content, d_out_latent)
            delta = jnp.sum(probs * d_probs, axis=0, keepdims=True)
            d_scores = (probs * (d_probs - delta) * inv_root).astype(bf16)
            d_full_t = dot(keys_t_ref[...], d_scores)
            d_absorbed_t = d_full_t[:rank].astype(bf16)
            d_nope_t = dot(w_uk, d_absorbed_t)
            dq_ref[:, head * width : (head + 1) * width] = jnp.concatenate(
                [d_nope_t, d_full_t[rank:]], axis=0
            ).T.astype(bf16)
            own[step, base : base + nope] = dot_t(q_nope.T, d_absorbed_t).astype(bf16)
            dkeys[:, :rank] += dot(d_scores, absorbed) + dot(low, d_out_latent)
            dkeys[:, rank:] += dot(d_scores, q_rope)
        pair_copy(step).start()

    @pl.when(step == steps - 1)
    def _():
        for back in range(SPAN + 1):
            sent[back] = dkeys[back * tok : (back + 1) * tok, :].astype(bf16)
        for d in range(1, peers):
            head_copy(d).start()

    at1 = step - LAGS[0]

    @pl.when((at1 >= 0) & (at1 < steps))
    def _():
        pair_copy(at1).wait()
        mine = own[at1, half_rows(parity)].astype(f32)
        mid[at1] = (mine + from_pair[at1].astype(f32)).astype(bf16)
        for d in range(1, line):
            line_copy(at1, d).start()

    at2 = step - LAGS[1]

    @pl.when((at2 >= 0) & (at2 < steps))
    def _():
        total = mid[at2, part_rows(place)].astype(f32)
        for d in range(1, line):
            line_copy(at2, d).wait()
            total = total + from_line[at2, d - 1].astype(f32)
        rows = pl.ds(pl.multiple_of(parity * half + place * part, 16), part)
        final[at2, rows] = total.astype(bf16)
        for d in range(1, line):
            back_copy(at2, d).start()

    at3 = step - LAGS[2]

    @pl.when((at3 >= 0) & (at3 < steps))
    def _():
        for d in range(1, line):
            back_copy(at3, d).wait()
        last_copy(at3).start()

    at4 = step - LAGS[3]

    @pl.when((at4 >= 0) & (at4 < steps))
    def _():
        last_copy(at4).wait()
        for head in range(PAIR):
            base = head * (nope + value)
            duk_ref[head] = final[at4, base : base + nope]
            duv_ref[head] = final[at4, base + nope : base + nope + value]

    own_rows = pl.ds(pl.multiple_of(head_me * quarter, 16), quarter)

    @pl.when(step == steps)
    def _():
        for d in range(1, peers):
            head_copy(d).wait()
        for back in range(1, SPAN + 1):
            block = sent[back, own_rows, :].astype(f32)
            for d in range(1, peers):
                block = block + from_head[d - 1, back].astype(f32)
            shifts[back - 1] = block.astype(bf16)

            @pl.when(me >= back)
            def _():
                ctx_copy(back).start()

        from_ctx_zero = jnp.zeros_like(from_ctx[0])
        for back in range(1, SPAN + 1):

            @pl.when(me + back >= n)
            def _():
                from_ctx[back - 1] = from_ctx_zero

    @pl.when(step == steps + 1)
    def _():
        block = sent[0, own_rows, :].astype(f32)
        for d in range(1, peers):
            block = block + from_head[d - 1, 0].astype(f32)
        for back in range(1, SPAN + 1):

            @pl.when(me >= back)
            def _():
                ctx_copy(back).wait_send()

            @pl.when(me + back < n)
            def _():
                ctx_copy(back).wait_recv()

            block = block + from_ctx[back - 1].astype(f32)
        gathered[own_rows] = block.astype(bf16)
        for d in range(1, peers):
            out_copy(d).start()

    @pl.when(step == steps + 3)
    def _():
        for d in range(1, peers):
            out_copy(d).wait()
        dlat_ref[...] = gathered[...]


def attend(n, peers, lat_t, bias, query, d_out, w_uk, w_uv):
    tok = query.shape[0]
    heads, nope, rank = w_uk.shape
    value = w_uv.shape[1]
    width = query.shape[1] // heads
    lat = lat_t.shape[0]
    span = bias.shape[0]
    steps = heads // PAIR
    rows = PAIR * (nope + value)
    half = rows // 2
    line = n // 2
    part = half // line
    quarter = tok // peers
    bf16 = jnp.bfloat16
    fixed = lambda i: (0, 0)
    columns = lambda i: (0, jnp.minimum(i, steps - 1))
    weight = lambda i: (jnp.minimum(i, steps - 1), 0, 0)
    late = lambda i: (jnp.maximum(i - LAGS[3], 0), 0, 0)
    flops = 2 * tok * heads * (span * (3 * lat + 3 * rank) + 6 * nope * rank)
    sem = pltpu.SemaphoreType.DMA
    return pl.pallas_call(
        functools.partial(
            attention_kernel, nope, width - nope, rank, value, steps, n, peers
        ),
        grid=(steps + LAGS[3],),
        in_specs=[
            pl.BlockSpec((lat, tok), fixed),
            pl.BlockSpec((span, tok), fixed),
            pl.BlockSpec((tok, PAIR * width), columns),
            pl.BlockSpec((tok, PAIR * value), columns),
            pl.BlockSpec((PAIR, nope, rank), weight),
            pl.BlockSpec((PAIR, value, rank), weight),
        ],
        out_specs=[
            pl.BlockSpec((tok, PAIR * value), columns),
            pl.BlockSpec((tok, PAIR * width), columns),
            pl.BlockSpec((tok, lat), fixed),
            pl.BlockSpec((PAIR, nope, rank), late),
            pl.BlockSpec((PAIR, value, rank), late),
        ],
        out_shape=[
            jax.ShapeDtypeStruct((tok, heads * value), bf16),
            jax.ShapeDtypeStruct((tok, heads * width), bf16),
            jax.ShapeDtypeStruct((tok, lat), bf16),
            jax.ShapeDtypeStruct((heads, nope, rank), bf16),
            jax.ShapeDtypeStruct((heads, value, rank), bf16),
        ],
        scratch_shapes=[
            pltpu.VMEM((span, lat), bf16),
            pltpu.VMEM((lat, span), bf16),
            pltpu.VMEM((span, lat), jnp.float32),
            pltpu.VMEM((steps, rows, rank), bf16),
            pltpu.VMEM((steps, half, rank), bf16),
            pltpu.VMEM((steps, half, rank), bf16),
            pltpu.VMEM((steps, line - 1, part, rank), bf16),
            pltpu.VMEM((steps, rows, rank), bf16),
            pltpu.VMEM((SPAN + 1, tok, lat), bf16),
            pltpu.VMEM((peers - 1, SPAN + 1, quarter, lat), bf16),
            pltpu.VMEM((SPAN, quarter, lat), bf16),
            pltpu.VMEM((SPAN, quarter, lat), bf16),
            pltpu.VMEM((tok, lat), bf16),
            sem((steps,)), sem((steps,)),
            sem((steps, line - 1)), sem((steps, line - 1)),
            sem((steps, line - 1)), sem((steps, line - 1)),
            sem((steps,)), sem((steps,)),
            sem((peers - 1,)), sem((peers - 1,)),
            sem((SPAN,)), sem((SPAN,)),
            sem((peers - 1,)), sem((peers - 1,)),
            sem((SPAN,)), sem((SPAN,)),
            sem((SPAN,)), sem((SPAN,)),
        ],
        compiler_params=pltpu.CompilerParams(
            vmem_limit_bytes=52 * 1024 * 1024, collective_id=0, has_side_effects=True
        ),
        cost_estimate=pl.CostEstimate(
            flops=flops, bytes_accessed=16 * span * lat, transcendentals=tok * heads * span
        ),
    )(lat_t, bias, query, d_out, w_uk, w_uv)


def mask_bias(tok, block_mask, segments):
    position = lax.axis_index("ctx")
    offsets = jnp.arange(tok, dtype=jnp.int32)
    seg_query = lax.dynamic_slice_in_dim(segments, position * tok, tok)
    parts = []
    for back in range(SPAN + 1):
        block = position - back
        clamped = jnp.maximum(block, 0)
        seg_key = lax.dynamic_slice_in_dim(segments, clamped * tok, tok)
        granted = block_mask[position, clamped] == 1
        allowed = (block >= 0) & ((seg_query[None, :] == seg_key[:, None]) | granted)
        if back == 0:
            allowed = allowed & (offsets[:, None] <= offsets[None, :])
        parts.append(jnp.where(allowed, 0.0, -jnp.inf).astype(jnp.float32))
    return jnp.concatenate(parts, axis=0)


def body(latent, query, d_out, w_uk, w_uv, block_mask, segments):
    tok = latent.shape[0]
    bias = mask_bias(tok, block_mask, segments)
    att, dq, d_latent, d_w_uk, d_w_uv = attend(
        lax.axis_size("ctx"), lax.axis_size("head"), latent.T, bias, query, d_out, w_uk, w_uv
    )
    wide = jnp.float32
    return att, dq, d_latent.astype(wide), d_w_uk.astype(wide), d_w_uv.astype(wide)


def solution(mesh):
    in_specs = (
        P("ctx", None),
        P("ctx", "head"),
        P("ctx", "head"),
        P("head", None, None),
        P("head", None, None),
        P(),
        P(),
    )
    out_specs = (
        P("ctx", "head"),
        P("ctx", "head"),
        P("ctx", None),
        P("head", None, None),
        P("head", None, None),
    )
    return jax.shard_map(body, mesh=mesh, in_specs=in_specs, out_specs=out_specs, check_vma=False)
```

```python
import functools
import math

import jax
import jax.numpy as jnp
from jax import lax
from jax.experimental import pallas as pl
from jax.experimental.pallas import tpu as pltpu
from jax.sharding import PartitionSpec as P

SPAN = 2
PAIR = 2


def dot(a, b):
    return lax.dot_general(a, b, (((1,), (0,)), ((), ())), preferred_element_type=jnp.float32)


def dot_t(a, b):
    return lax.dot_general(a, b, (((1,), (1,)), ((), ())), preferred_element_type=jnp.float32)


def attention_kernel(
    nope, rope, rank, value, steps, n, peers, bits,
    lat_t_ref, bias_ref, query_ref, grads_ref, uk_ref, uv_ref,
    att_ref, dq_ref, dlat_ref, duk_ref, duv_ref,
    keys_ref, keys_t_ref, dkeys, own, landing, final, sent, from_head, shifts, from_ctx, gathered,
    sum_send, sum_recv,
    head_send, head_recv, ctx_send, ctx_recv, out_send, out_recv, key_send, key_recv,
    share_send, share_recv,
):
    bf16, f32 = jnp.bfloat16, jnp.float32
    width = nope + rope
    inv_root = 1.0 / math.sqrt(width)
    to_log2 = inv_root * math.log2(math.e)
    step = pl.program_id(0)
    me = lax.axis_index("ctx")
    head_me = lax.axis_index("head")
    rows = own.shape[1]
    tok = att_ref.shape[0]
    quarter = tok // peers

    def remote(src, dst, send, recv, target):
        return pltpu.make_async_remote_copy(
            src_ref=src, dst_ref=dst, send_sem=send, recv_sem=recv,
            device_id=target, device_id_type=pl.DeviceIdType.MESH,
        )

    def stage(c, k):
        turned = (lax.rem(c + 4, 8) + 1) // 8
        stride = 2**k + turned * (2 ** ((k + 1) % bits) - 2**k)
        return stride, lax.rem(me // stride, 2)

    def partner(c, k):
        stride, bit = stage(c, k)
        return {"ctx": me + (1 - 2 * bit) * stride}

    def offset(c, k):
        at = 0
        for j in range(k):
            at = at + stage(c, j)[1] * (rows >> (j + 1))
        return at

    def region(at, k):
        return pl.ds(pl.multiple_of(at, 16), rows >> k)

    def landed(k):
        return pl.ds(rows - (rows >> k), rows >> (k + 1))

    def sum_copy(c, k):
        other = offset(c, k) + (1 - stage(c, k)[1]) * (rows >> (k + 1))
        return remote(
            own.at[c, region(other, k + 1)], landing.at[c, landed(k)],
            sum_send.at[c, k], sum_recv.at[c, k], partner(c, k),
        )

    def back_copy(c, k):
        part = final.at[c, region(offset(c, k + 1), k + 1)]
        return remote(
            part, part, sum_send.at[c, bits + k], sum_recv.at[c, bits + k], partner(c, k)
        )

    def head_copy(d):
        peer = lax.rem(head_me + d, peers)
        rows = pl.ds(pl.multiple_of(peer * quarter, 16), quarter)
        return remote(
            sent.at[:, rows, :], from_head.at[d - 1],
            head_send.at[d - 1], head_recv.at[d - 1], {"head": peer},
        )

    def ctx_copy(d):
        return remote(
            shifts.at[d - 1], from_ctx.at[d - 1],
            ctx_send.at[d - 1], ctx_recv.at[d - 1], {"ctx": lax.rem(me - d + n, n)},
        )

    def out_copy(d):
        peer = lax.rem(head_me + d, peers)
        rows = pl.ds(pl.multiple_of(head_me * quarter, 16), quarter)
        return remote(
            gathered.at[rows], gathered.at[rows],
            out_send.at[d - 1], out_recv.at[d - 1], {"head": peer},
        )

    core = lax.rem(head_me, 2)
    core_half = keys_t_ref.shape[0] // 2
    core_rows = pl.ds(pl.multiple_of(core * core_half, 16), core_half)

    def key_copy(d):
        return remote(
            keys_t_ref.at[core_rows, :tok], keys_t_ref.at[core_rows, d * tok : (d + 1) * tok],
            key_send.at[d - 1], key_recv.at[d - 1], {"ctx": lax.rem(me + d, n)},
        )

    def share_copy(d):
        block = keys_t_ref.at[core_rows, d * tok : (d + 1) * tok]
        return remote(
            block, block, share_send.at[d - 1], share_recv.at[d - 1],
            {"head": head_me + 1 - 2 * core},
        )

    @pl.when(step == 0)
    def _():
        barrier = pltpu.get_barrier_semaphore()
        for d in range(1, n):
            pl.semaphore_signal(
                barrier, inc=1, device_id={"ctx": lax.rem(me + d, n)},
                device_id_type=pl.DeviceIdType.MESH,
            )
        for d in range(1, peers):
            pl.semaphore_signal(
                barrier, inc=1, device_id={"head": lax.rem(head_me + d, peers)},
                device_id_type=pl.DeviceIdType.MESH,
            )
        keys_t_ref[:, :tok] = lat_t_ref[...]
        pl.semaphore_wait(barrier, n - 1 + peers - 1)
        for d in range(1, SPAN + 1):

            @pl.when(me + d < n)
            def _():
                key_copy(d).start()

            @pl.when(me < d)
            def _():
                keys_t_ref[:, d * tok : (d + 1) * tok] = jnp.zeros(
                    (keys_t_ref.shape[0], tok), keys_t_ref.dtype
                )

        dkeys[...] = jnp.zeros_like(dkeys)
        keys_ref[:tok, :] = lat_t_ref[...].T
        for d in range(1, SPAN + 1):

            @pl.when(me >= d)
            def _():
                key_copy(d).wait_recv()
                share_copy(d).start()

        for d in range(1, SPAN + 1):

            @pl.when(me >= d)
            def _():
                share_copy(d).wait()

            keys_ref[d * tok : (d + 1) * tok, :] = keys_t_ref[:, d * tok : (d + 1) * tok].T
        for d in range(1, SPAN + 1):

            @pl.when(me + d < n)
            def _():
                key_copy(d).wait_send()

    @pl.when(step < steps)
    def _():
        queries = query_ref[...]
        for head in range(PAIR):
            q_nope = queries[:, head * width : head * width + nope]
            q_rope = queries[:, head * width + nope : (head + 1) * width]
            grads = grads_ref[:, head * value : (head + 1) * value]
            w_uk = uk_ref[head]
            w_uv = uv_ref[head]
            base = head * (nope + value)
            absorbed = dot(q_nope, w_uk).astype(bf16)
            d_out_latent = dot(grads, w_uv).astype(bf16)
            content = keys_ref[:, :rank]
            scores = dot_t(content, absorbed) + dot_t(keys_ref[:, rank:], q_rope)
            scores = scores * to_log2 + bias_ref[...]
            weights = jnp.exp2(scores - jnp.max(scores, axis=0, keepdims=True))
            probs = weights * (1.0 / jnp.sum(weights, axis=0, keepdims=True))
            low = probs.astype(bf16)
            out_t = dot(keys_t_ref[:rank, :], low).astype(bf16)
            att_t = dot(w_uv, out_t)
            att_ref[:, head * value : (head + 1) * value] = att_t.T.astype(bf16)
            own[step, base + nope : base + nope + value] = dot_t(grads.T, out_t).astype(bf16)
            d_probs = dot_t(content, d_out_latent)
            delta = jnp.sum(probs * d_probs, axis=0, keepdims=True)
            d_scores = (probs * (d_probs - delta) * inv_root).astype(bf16)
            d_full_t = dot(keys_t_ref[...], d_scores)
            d_absorbed_t = d_full_t[:rank].astype(bf16)
            d_nope_t = dot(w_uk, d_absorbed_t)
            dq_ref[:, head * width : (head + 1) * width] = jnp.concatenate(
                [d_nope_t, d_full_t[rank:]], axis=0
            ).T.astype(bf16)
            own[step, base : base + nope] = dot_t(q_nope.T, d_absorbed_t).astype(bf16)
            dkeys[:, :rank] += dot(d_scores, absorbed) + dot(low, d_out_latent)
            dkeys[:, rank:] += dot(d_scores, q_rope)
        sum_copy(step, 0).start()

    @pl.when(step == steps - 1)
    def _():
        for back in range(SPAN + 1):
            sent[back] = dkeys[back * tok : (back + 1) * tok, :].astype(bf16)
        for d in range(1, peers):
            head_copy(d).start()

    for k in range(bits):
        at = step - 1 - k

        @pl.when((at >= 0) & (at < steps))
        def _():
            sum_copy(at, k).wait()
            mine = region(offset(at, k + 1), k + 1)
            total = own[at, mine].astype(f32) + landing[at, landed(k)].astype(f32)
            if k + 1 < bits:
                own[at, mine] = total.astype(bf16)
                sum_copy(at, k + 1).start()
            else:
                final[at, mine] = total.astype(bf16)
                back_copy(at, k).start()

    for k in range(bits - 1, -1, -1):
        at = step - 2 * bits + k

        @pl.when((at >= 0) & (at < steps))
        def _():
            back_copy(at, k).wait()
            if k > 0:
                back_copy(at, k - 1).start()
            else:
                for head in range(PAIR):
                    base = head * (nope + value)
                    duk_ref[head] = final[at, base : base + nope]
                    duv_ref[head] = final[at, base + nope : base + nope + value]

    own_rows = pl.ds(pl.multiple_of(head_me * quarter, 16), quarter)

    @pl.when(step == steps)
    def _():
        for d in range(1, peers):
            head_copy(d).wait()
        for back in range(1, SPAN + 1):
            block = sent[back, own_rows, :].astype(f32)
            for d in range(1, peers):
                block = block + from_head[d - 1, back].astype(f32)
            shifts[back - 1] = block.astype(bf16)

            @pl.when(me >= back)
            def _():
                ctx_copy(back).start()

        from_ctx_zero = jnp.zeros_like(from_ctx[0])
        for back in range(1, SPAN + 1):

            @pl.when(me + back >= n)
            def _():
                from_ctx[back - 1] = from_ctx_zero

    @pl.when(step == steps + 1)
    def _():
        block = sent[0, own_rows, :].astype(f32)
        for d in range(1, peers):
            block = block + from_head[d - 1, 0].astype(f32)
        for back in range(1, SPAN + 1):

            @pl.when(me >= back)
            def _():
                ctx_copy(back).wait_send()

            @pl.when(me + back < n)
            def _():
                ctx_copy(back).wait_recv()

            block = block + from_ctx[back - 1].astype(f32)
        gathered[own_rows] = block.astype(bf16)
        for d in range(1, peers):
            out_copy(d).start()

    @pl.when(step == steps + 3)
    def _():
        for d in range(1, peers):
            out_copy(d).wait()
        dlat_ref[...] = gathered[...]


def attend(n, peers, lat_t, bias, query, d_out, w_uk, w_uv):
    tok = query.shape[0]
    heads, nope, rank = w_uk.shape
    value = w_uv.shape[1]
    width = query.shape[1] // heads
    lat = lat_t.shape[0]
    span = bias.shape[0]
    steps = heads // PAIR
    rows = PAIR * (nope + value)
    bits = n.bit_length() - 1
    lag = 2 * bits
    quarter = tok // peers
    bf16 = jnp.bfloat16
    fixed = lambda i: (0, 0)
    columns = lambda i: (0, jnp.minimum(i, steps - 1))
    weight = lambda i: (jnp.minimum(i, steps - 1), 0, 0)
    late = lambda i: (jnp.maximum(i - lag, 0), 0, 0)
    flops = 2 * tok * heads * (span * (3 * lat + 3 * rank) + 6 * nope * rank)
    sem = pltpu.SemaphoreType.DMA
    return pl.pallas_call(
        functools.partial(
            attention_kernel, nope, width - nope, rank, value, steps, n, peers, bits
        ),
        grid=(steps + lag,),
        in_specs=[
            pl.BlockSpec((lat, tok), fixed),
            pl.BlockSpec((span, tok), fixed),
            pl.BlockSpec((tok, PAIR * width), columns),
            pl.BlockSpec((tok, PAIR * value), columns),
            pl.BlockSpec((PAIR, nope, rank), weight),
            pl.BlockSpec((PAIR, value, rank), weight),
        ],
        out_specs=[
            pl.BlockSpec((tok, PAIR * value), columns),
            pl.BlockSpec((tok, PAIR * width), columns),
            pl.BlockSpec((tok, lat), fixed),
            pl.BlockSpec((PAIR, nope, rank), late),
            pl.BlockSpec((PAIR, value, rank), late),
        ],
        out_shape=[
            jax.ShapeDtypeStruct((tok, heads * value), bf16),
            jax.ShapeDtypeStruct((tok, heads * width), bf16),
            jax.ShapeDtypeStruct((tok, lat), bf16),
            jax.ShapeDtypeStruct((heads, nope, rank), bf16),
            jax.ShapeDtypeStruct((heads, value, rank), bf16),
        ],
        scratch_shapes=[
            pltpu.VMEM((span, lat), bf16),
            pltpu.VMEM((lat, span), bf16),
            pltpu.VMEM((span, lat), jnp.float32),
            pltpu.VMEM((steps, rows, rank), bf16),
            pltpu.VMEM((steps, rows, rank), bf16),
            pltpu.VMEM((steps, rows, rank), bf16),
            pltpu.VMEM((SPAN + 1, tok, lat), bf16),
            pltpu.VMEM((peers - 1, SPAN + 1, quarter, lat), bf16),
            pltpu.VMEM((SPAN, quarter, lat), bf16),
            pltpu.VMEM((SPAN, quarter, lat), bf16),
            pltpu.VMEM((tok, lat), bf16),
            sem((steps, lag)), sem((steps, lag)),
            sem((peers - 1,)), sem((peers - 1,)),
            sem((SPAN,)), sem((SPAN,)),
            sem((peers - 1,)), sem((peers - 1,)),
            sem((SPAN,)), sem((SPAN,)),
            sem((SPAN,)), sem((SPAN,)),
        ],
        compiler_params=pltpu.CompilerParams(
            vmem_limit_bytes=52 * 1024 * 1024, collective_id=0, has_side_effects=True
        ),
        cost_estimate=pl.CostEstimate(
            flops=flops, bytes_accessed=16 * span * lat, transcendentals=tok * heads * span
        ),
    )(lat_t, bias, query, d_out, w_uk, w_uv)


def mask_bias(tok, block_mask, segments):
    position = lax.axis_index("ctx")
    offsets = jnp.arange(tok, dtype=jnp.int32)
    seg_query = lax.dynamic_slice_in_dim(segments, position * tok, tok)
    parts = []
    for back in range(SPAN + 1):
        block = position - back
        clamped = jnp.maximum(block, 0)
        seg_key = lax.dynamic_slice_in_dim(segments, clamped * tok, tok)
        granted = block_mask[position, clamped] == 1
        allowed = (block >= 0) & ((seg_query[None, :] == seg_key[:, None]) | granted)
        if back == 0:
            allowed = allowed & (offsets[:, None] <= offsets[None, :])
        parts.append(jnp.where(allowed, 0.0, -jnp.inf).astype(jnp.float32))
    return jnp.concatenate(parts, axis=0)


def body(latent, query, d_out, w_uk, w_uv, block_mask, segments):
    tok = latent.shape[0]
    bias = mask_bias(tok, block_mask, segments)
    att, dq, d_latent, d_w_uk, d_w_uv = attend(
        lax.axis_size("ctx"), lax.axis_size("head"), latent.T, bias, query, d_out, w_uk, w_uv
    )
    wide = jnp.float32
    return att, dq, d_latent.astype(wide), d_w_uk.astype(wide), d_w_uv.astype(wide)


def solution(mesh):
    in_specs = (
        P("ctx", None),
        P("ctx", "head"),
        P("ctx", "head"),
        P("head", None, None),
        P("head", None, None),
        P(),
        P(),
    )
    out_specs = (
        P("ctx", "head"),
        P("ctx", "head"),
        P("ctx", None),
        P("head", None, None),
        P("head", None, None),
    )
    return jax.shard_map(body, mesh=mesh, in_specs=in_specs, out_specs=out_specs, check_vma=False)
```
